32 devices in a mesh: sec: 4 (over y, x), feat: 2 (over core), row: 4 (over z).
Axes of the slice: x: 2, y: 2, z: 4, core: 2. Of those that a mesh axis runs over, the one named last changes fastest.
Arguments:
- inputs: bfloat16 [4, 1024, 2304], P('sec', 'row', 'feat'), may hold values from -6 to 6
- enc_weight: bfloat16 [4, 2304, 16384], P('sec', None, 'feat'), may hold values from -0.125 to 0.125
- enc_bias: float32 [4, 16384], P('sec', 'feat'), may hold values from -0.5 to 0.5
- dec_weight: bfloat16 [4, 4, 16384, 2304], P('sec', None, 'feat', 'row'), may hold values from -0.046875 to 0.046875
- dec_bias: float32 [4, 2304], P('sec', 'row'), may hold values from -3 to 3
Outputs:
- recon: bfloat16 [4, 1024, 2304], P('sec', 'feat', 'row')
The draws below stay inside these ranges and needn't reach their ends.
All inputs are finite; a program needn't handle non-finite values.
Results may differ from the reference program's by a relative error of at most 0.0047.
Values may be sent and summed in bfloat16 or wider, within the bound.
A program may use at most 256 MiB of HBM per device.

```python
import jax
import jax.numpy as jnp

D = 2304
F = 16384
S = 4
TOKENS = 1024


def level_of(own_key, shape, pieces, low, largest):
    gain = 1.0
    for dim, shards_of in pieces:
        steps = jax.random.uniform(jax.random.fold_in(jax.random.fold_in(own_key, 6), dim), (shards_of,), jnp.float32, low / len(pieces), largest / len(pieces))
        gain = gain * jnp.repeat(jnp.exp(steps), shape[dim] // shards_of).reshape((-1,) + (1,) * (len(shape) - 1 - dim))
    return gain


def gaussian(stream_key, dims, deviation, most, shards=(), dtype=jnp.bfloat16):
    result = jax.random.normal(stream_key, dims, jnp.float32) * deviation
    if len(shards) > 0:
        result = level_of(stream_key, dims, shards, -0.22, 0.18) * result
    return jnp.clip(result, min=-most, max=most).astype(dtype)


def setup_inputs(seed: int = 0) -> dict:
    seeds = jax.random.split(jax.random.key(seed), 6)
    inputs = gaussian(seeds[0], (S, TOKENS, D), 1.0, 6.0, ((0, 4), (1, 4), (2, 2)))
    enc_weight = gaussian(seeds[1], (S, D, F), D ** -0.5, 0.125, ((0, 4), (2, 2)))
    enc_bias = jnp.clip(jax.random.uniform(seeds[2], (S, F), jnp.float32, -0.5, 0.5) * level_of(seeds[2], (S, F), ((0, 4), (1, 2)), -0.4, 0.0), -0.5, 0.5)
    dec_weight = gaussian(seeds[3], (S, S, F, D), F ** -0.5, 0.046875, ((0, 4), (2, 2), (3, 4)))
    dec_bias = gaussian(seeds[4], (S, D), 0.5, 3.0, ((0, 4), (1, 4)), jnp.float32)
    return dict(inputs=inputs, enc_weight=enc_weight, enc_bias=enc_bias, dec_weight=dec_weight, dec_bias=dec_bias)


def reference(inputs, enc_weight, enc_bias, dec_weight, dec_bias):
    features = []
    for source in range(S):
        hidden = jnp.dot(inputs[source], enc_weight[source], preferred_element_type=jnp.float32) + enc_bias[source]
        features.append(jnp.maximum(hidden, 0.0).astype(jnp.bfloat16))
    results = []
    for target in range(S):
        totals = jnp.zeros((TOKENS, D), jnp.float32)
        for source in range(target + 1):
            totals = totals + jnp.dot(features[source], dec_weight[target, source], preferred_element_type=jnp.float32)
        results.append((totals + dec_bias[target]).astype(jnp.bfloat16))
    return jnp.stack(results)
```

```python
import jax
import jax.numpy as jnp
from jax import lax
from jax.sharding import PartitionSpec as P


def pairs_of(sections):
    step = 1
    while step < sections:
        step *= 2
    rounds = []
    for flip in range(1, step):
        pairs = [(s, s ^ flip) for s in range(sections) if s < (s ^ flip) < sections]
        rounds.append((flip, pairs))
    return rounds


def gather_feat(block, shards):
    if shards != 2:
        return lax.all_gather(block, "feat", axis=1, tiled=True)
    other = lax.ppermute(block, "feat", [(0, 1), (1, 0)])
    first = lax.axis_index("feat") == 0
    return jnp.where(
        first,
        jnp.concatenate([block, other], axis=1),
        jnp.concatenate([other, block], axis=1),
    )


def scatter_sum_feat(total, shards):
    if shards != 2:
        return lax.psum_scatter(total, "feat", scatter_dimension=0, tiled=True)
    half = total.shape[0] // 2
    me = lax.axis_index("feat")
    give = lax.dynamic_slice_in_dim(total, (1 - me) * half, half, 0)
    keep = lax.dynamic_slice_in_dim(total, me * half, half, 0)
    return keep + lax.ppermute(give, "feat", [(0, 1), (1, 0)])


def dot(a, b):
    return jnp.dot(a, b, preferred_element_type=jnp.float32)


def per_device(sections, shards, inputs, enc_weight, enc_bias, dec_weight, dec_bias):
    encoder, bias, decoders = enc_weight[0], enc_bias[0], dec_weight[0]
    depth = encoder.shape[1]
    me = lax.axis_index("sec")
    rounds = pairs_of(sections)
    end_z = depth * 7 // 32
    end_a = depth * 13 // 32

    def encode(rows, low, high):
        hidden = dot(rows, encoder[:, low:high])
        return jnp.maximum(hidden + bias[low:high], 0.0).astype(jnp.bfloat16)

    def decoder(source, low, high):
        return lax.dynamic_slice(
            decoders, (source, low, 0), (1, high - low, decoders.shape[2])
        )[0]

    lent = []
    for flip, pairs in reversed(rounds):
        mine = decoder(jnp.minimum(me ^ flip, sections - 1), end_a, depth)
        lent.append(lax.ppermute(mine, "sec", [(hi, lo) for lo, hi in pairs]))

    rows_z = encode(gather_feat(inputs[0], shards), 0, end_z)
    near = [lax.ppermute(rows_z, "sec", pairs) for _, pairs in reversed(rounds)]
    every = gather_feat(lax.all_gather(inputs[0], "row", axis=0, tiled=True), shards)
    feats_a = encode(every, end_z, end_a)
    direct = [lax.ppermute(feats_a, "sec", pairs) for _, pairs in reversed(rounds)]
    gathered = [lax.all_gather(block, "row", axis=0, tiled=True) for block in near]
    feats_z = encode(every, 0, end_z)
    feats_w = encode(every, end_a, depth)

    total = dot(feats_z, decoder(me, 0, end_z))
    total += dot(feats_a, decoder(me, end_z, end_a))
    total += dot(feats_w, decoder(me, end_a, depth))
    returned = 0.0
    for i, (flip, pairs) in enumerate(reversed(rounds)):
        source = jnp.minimum(me ^ flip, sections - 1)
        part = scatter_sum_feat(dot(feats_w, lent[i]), shards)
        back = lax.ppermute(part.astype(jnp.bfloat16), "sec", pairs)
        returned = returned + back.astype(jnp.float32)
        total += dot(gathered[i], decoder(source, 0, end_z))
        total += dot(direct[i], decoder(source, end_z, end_a))
    summed = scatter_sum_feat(total, shards) + returned
    return (summed + dec_bias[0]).astype(jnp.bfloat16)[None]


def solution(mesh):
    sections, shards = mesh.shape["sec"], mesh.shape["feat"]
    in_specs = (
        P("sec", "row", "feat"),
        P("sec", None, "feat"),
        P("sec", "feat"),
        P("sec", None, "feat", "row"),
        P("sec", "row"),
    )
    out_specs = P("sec", "feat", "row")

    def per_shard(*arrays):
        return per_device(sections, shards, *arrays)

    return jax.shard_map(
        per_shard, mesh=mesh, in_specs=in_specs, out_specs=out_specs, check_vma=False
    )
```

```python
import jax
import jax.numpy as jnp
from jax import lax
from jax.sharding import PartitionSpec as P


def pairs_of(sections):
    step = 1
    while step < sections:
        step *= 2
    rounds = []
    for flip in range(1, step):
        pairs = [(s, s ^ flip) for s in range(sections) if s < (s ^ flip) < sections]
        rounds.append((flip, pairs))
    return rounds


def gather_feat(block, shards):
    if shards != 2:
        return lax.all_gather(block, "feat", axis=1, tiled=True)
    other = lax.ppermute(block, "feat", [(0, 1), (1, 0)])
    first = lax.axis_index("feat") == 0
    return jnp.where(
        first,
        jnp.concatenate([block, other], axis=1),
        jnp.concatenate([other, block], axis=1),
    )


def scatter_sum_feat(total, shards):
    if shards != 2:
        return lax.psum_scatter(total, "feat", scatter_dimension=0, tiled=True)
    half = total.shape[0] // 2
    me = lax.axis_index("feat")
    give = lax.dynamic_slice_in_dim(total, (1 - me) * half, half, 0)
    keep = lax.dynamic_slice_in_dim(total, me * half, half, 0)
    return keep + lax.ppermute(give, "feat", [(0, 1), (1, 0)])


def dot(a, b):
    return jnp.dot(a, b, preferred_element_type=jnp.float32)


def after(value, *earlier):
    return lax.optimization_barrier((value, *earlier))[0]


def per_device(sections, shards, inputs, enc_weight, enc_bias, dec_weight, dec_bias):
    encoder, bias, decoders = enc_weight[0], enc_bias[0], dec_weight[0]
    depth = encoder.shape[1]
    me = lax.axis_index("sec")
    rounds = pairs_of(sections)
    end_z = depth * 6 // 32
    end_a = depth * 12 // 32
    middle = (end_a + depth) // 2

    def encode(rows, low, high):
        hidden = dot(rows, encoder[:, low:high])
        return jnp.maximum(hidden + bias[low:high], 0.0).astype(jnp.bfloat16)

    def decoder(source, low, high):
        return lax.dynamic_slice(
            decoders, (source, low, 0), (1, high - low, decoders.shape[2])
        )[0]

    rounds = rounds[::-1]
    sources = [jnp.minimum(me ^ flip, sections - 1) for flip, _ in rounds]

    def lend(i, low, high, *earlier):
        mine = after(decoder(sources[i], low, high), *earlier)
        return lax.ppermute(mine, "sec", [(hi, lo) for lo, hi in rounds[i][1]])

    first = lend(0, end_a, middle)
    rows_z = encode(gather_feat(inputs[0], shards), 0, end_z)
    near = [lax.ppermute(rows_z, "sec", pairs) for _, pairs in rounds]
    every = gather_feat(lax.all_gather(inputs[0], "row", axis=0, tiled=True), shards)
    every = after(every, first)
    second = lend(0, middle, depth, first)
    feats_a = encode(every, end_z, end_a)
    direct = [lax.ppermute(feats_a, "sec", pairs) for _, pairs in rounds]
    gathered = [lax.all_gather(block, "row", axis=0, tiled=True) for block in near]
    feats_w = encode(every, end_a, depth)
    feats_z = encode(every, 0, end_z)

    def give_back(i, parts):
        part = scatter_sum_feat(parts, shards)
        back = lax.ppermute(part.astype(jnp.bfloat16), "sec", rounds[i][1])
        return back.astype(jnp.float32)

    cut = middle - end_a
    feats_w = after(feats_w, second)
    rest = [lend(i, end_a, depth, second) for i in range(1, len(rounds))]
    returned = give_back(
        0, dot(feats_w[:, :cut], first) + dot(feats_w[:, cut:], second)
    )
    total = dot(feats_z, decoder(me, 0, end_z))
    total += dot(feats_a, decoder(me, end_z, end_a))
    total += dot(feats_w, decoder(me, end_a, depth))
    for i, source in enumerate(sources):
        total += dot(gathered[i], decoder(source, 0, end_z))
        total += dot(direct[i], decoder(source, end_z, end_a))
    feats_w = after(feats_w, total)
    for i in range(1, len(rounds)):
        returned = returned + give_back(i, dot(feats_w, rest[i - 1]))
    summed = scatter_sum_feat(total, shards) + returned
    return (summed + dec_bias[0]).astype(jnp.bfloat16)[None]


def solution(mesh):
    sections, shards = mesh.shape["sec"], mesh.shape["feat"]
    in_specs = (
        P("sec", "row", "feat"),
        P("sec", None, "feat"),
        P("sec", "feat"),
        P("sec", None, "feat", "row"),
        P("sec", "row"),
    )
    out_specs = P("sec", "feat", "row")

    def per_shard(*arrays):
        return per_device(sections, shards, *arrays)

    return jax.shard_map(
        per_shard, mesh=mesh, in_specs=in_specs, out_specs=out_specs, check_vma=False
    )
```
